32 devices in a mesh: segment: 4 (over x, core), field: 4 (over z), row: 2 (over y).
Axes of the slice: x: 2, y: 2, z: 4, core: 2. Of those that a mesh axis runs over, the one named last changes fastest.
Arguments:
- embeddings: bfloat16 [4, 256, 64, 256], P('segment', 'row', 'field'), may hold values from -6 to 6
- compress: bfloat16 [4, 64, 8], P('segment'), may hold values from -1.5 to 1.5
- mixing: bfloat16 [4, 512, 16384], P('segment', None, ('field', 'row')), may hold values from -0.25 to 0.25
- rescale_factor: float32 [4, 64, 256], P('segment', 'field'), may hold values from 0.5 to 1.5
- active_block_flags: int32 [4, 3], P('field'), may hold values from 1 to 3
Outputs:
- handed_on: bfloat16 [4, 256, 64, 256], P('segment', 'row', 'field')
The draws below stay inside these ranges and needn't reach their ends.
All inputs are finite; a program needn't handle non-finite values.
Results may differ from the reference program's by a relative error of at most 0.013.
Values may be sent and summed in bfloat16 or wider, within the bound.
A program may use at most 128 MiB of HBM per device.

```python
import math
import jax
import jax.numpy as jnp
from jax import lax

E = 256
FIELD_DEV = 16
RANK = 8
ROWS = 256
FEATURE_COUNT = 64
RELAY_SECTIONS = 4
N_FIELD = 4


def plant(values, rng, low, top_value):
    index_at = [jax.random.randint(jax.random.fold_in(rng, axis), (), 0, length) for axis, length in enumerate(values.shape)]
    main_axis = values.shape.index(max(values.shape))
    neighbour = index_at[:main_axis] + [(index_at[main_axis] + 1) % values.shape[main_axis]] + index_at[main_axis + 1:]
    return values.at[tuple(index_at)].set(low).at[tuple(neighbour)].set(top_value)


def steps_of(rng, dims, shards, least, largest):
    level = 1.0
    for axis_at, blocks in shards:
        draws = jax.random.uniform(jax.random.fold_in(jax.random.fold_in(rng, 6), axis_at), (blocks,), jnp.float32, least / len(shards), largest / len(shards))
        level = level * jnp.repeat(jnp.exp(draws), dims[axis_at] // blocks).reshape((-1,) + (1,) * (len(dims) - 1 - axis_at))
    return level


def normal_values(key, dims, width, most, pieces=(), dtype=jnp.bfloat16):
    drawn = jax.random.normal(key, dims, jnp.float32) * width
    if len(pieces) > 0:
        drawn = steps_of(key, dims, pieces, -0.22, 0.18) * drawn
    return jnp.clip(drawn, min=-most, max=most).astype(dtype)


def setup_inputs(seed: int = 0) -> dict:
    key_of = jax.random.split(jax.random.key(seed), 6)
    return {
        "embeddings": normal_values(key_of[0], (RELAY_SECTIONS, ROWS, FEATURE_COUNT, E), 1.0, 6.0, ((0, 4), (1, 2), (2, 4))),
        "compress": normal_values(key_of[1], (RELAY_SECTIONS, FEATURE_COUNT, RANK), FIELD_DEV ** -0.5, 1.5, ((0, 4),)),
        "mixing": normal_values(key_of[2], (RELAY_SECTIONS, FEATURE_COUNT * RANK, FEATURE_COUNT * E), (FEATURE_COUNT * RANK) ** -0.5, 0.25, ((0, 4), (2, 8))),
        "rescale_factor": jnp.clip(1.0 + 0.1 * jax.random.normal(key_of[3], (RELAY_SECTIONS, FEATURE_COUNT, E), jnp.float32), 0.5, 1.5),
        "active_block_flags": plant(jax.random.randint(key_of[4], (N_FIELD, 3), 1, 4), jax.random.fold_in(key_of[4], 1), 1, 3).astype(jnp.int32),
    }


def one_section(section_panels, section_compress, section_mixing, section_gain, active_block_flags):
    shaped = section_panels.reshape(ROWS, N_FIELD, FIELD_DEV, E).astype(jnp.float32)
    compress_f = section_compress.reshape(N_FIELD, FIELD_DEV, RANK).astype(jnp.float32)
    reduced = jnp.einsum('bak,rbae->rbke', compress_f, shaped).astype(jnp.bfloat16)
    reduced = lax.optimization_barrier(reduced).astype(jnp.float32)
    block_activity = active_block_flags.astype(jnp.float32)
    pairwise_feature_product = jnp.zeros((ROWS, N_FIELD, FIELD_DEV, RANK), jnp.float32)
    for offset_ordinal in range(3):
        partner = jnp.roll(reduced, 1 - offset_ordinal, axis=1)
        lone_block_product = jnp.einsum('rbae,rbke->rbak', shaped, partner)
        pairwise_feature_product = pairwise_feature_product + block_activity[:, offset_ordinal][None, :, None, None] * lone_block_product
    scaled = (pairwise_feature_product * (1.0 / math.sqrt(E))).astype(jnp.bfloat16).reshape(ROWS, FEATURE_COUNT * RANK)
    mixed = jnp.dot(scaled, section_mixing, preferred_element_type=jnp.float32).astype(jnp.bfloat16)
    mixed = lax.optimization_barrier(mixed).astype(jnp.float32).reshape(ROWS, FEATURE_COUNT, E)
    summed = section_panels.astype(jnp.float32) + mixed
    mean_square = lax.optimization_barrier(jnp.mean(summed * summed, axis=-1, keepdims=True))
    return (summed * lax.rsqrt(mean_square + 1e-06) * section_gain[None]).astype(jnp.bfloat16)

def reference(embeddings, compress, mixing, rescale_factor, active_block_flags):
    outputs = []
    for section in range(RELAY_SECTIONS):
        outputs.append(one_section(embeddings[section], compress[section], mixing[section], rescale_factor[section], active_block_flags))
    stacked = jnp.stack(outputs)
    return jnp.roll(stacked, 1, axis=0)
```

```python
import functools
import math

import jax
import jax.numpy as jnp
from jax import lax
from jax.experimental import pallas as pl
from jax.experimental.pallas import tpu as pltpu
from jax.sharding import PartitionSpec as P

MESH = pl.DeviceIdType.MESH
BF16, F32 = jnp.bfloat16, jnp.float32


def dot(a, b, dims=((1,), (0,))):
    return lax.dot_general(a, b, (dims, ((), ())), preferred_element_type=F32)


def grid_of(shape):
    return (
        lax.broadcasted_iota(jnp.int32, shape, 0),
        lax.broadcasted_iota(jnp.int32, shape, 1),
    )


def kernel(
    sizes,
    emb_hbm, compress_ref, mix_hbm, gain_ref, flags_ref,
    out_ref,
    emb, mix, own, near, inter, gathered, mixed, back, spread, done,
    emb_sem, mix_sem,
    near_send, near_recv,
    gat_send, gat_recv,
    back_send, back_recv,
    out_send, out_recv,
):
    segments, owners, groups, rows, fields, width, rank, chunks, group = sizes
    seg = lax.axis_index("segment")
    fld = lax.axis_index("field")
    row = lax.axis_index("row")
    part = rows // chunks
    span = fields * rank
    each = fields // groups
    blocks = part // group
    before, after = lax.rem(fld + owners - 1, owners), lax.rem(fld + 1, owners)

    loads = []
    for c in range(chunks):
        rng = pl.ds(c * part * fields, part * fields)
        load = pltpu.make_async_copy(emb_hbm.at[rng], emb.at[rng], emb_sem.at[c])
        load.start()
        loads.append(load)
    mix_load = pltpu.make_async_copy(mix_hbm, mix, mix_sem)
    mix_load.start()

    barrier = pltpu.get_barrier_semaphore()
    peers = []
    for i in range(owners):
        for j in range(groups):
            if i or j:
                peers.append((seg, lax.rem(fld + i, owners), lax.rem(row + j, groups)))
    for peer in peers:
        pl.semaphore_signal(barrier, inc=1, device_id=peer, device_id_type=MESH)
    ahead = (lax.rem(seg + 1, segments), fld, row)
    behind = (lax.rem(seg + segments - 1, segments), fld, row)
    for peer in (ahead, behind):
        pl.semaphore_signal(barrier, inc=1, device_id=peer, device_id_type=MESH)

    start = pl.multiple_of(fld * fields, fields)
    block_weights = compress_ref[pl.ds(start, fields), :]
    a, b = grid_of((group * rank, rank))
    tall = dot((a % rank == b).astype(BF16), block_weights, ((1,), (1,))).astype(BF16)
    a, b = grid_of((fields, group * fields))
    wide = dot(tall, (b % fields == a).astype(BF16))
    a, b = grid_of((group * rank, group * fields))
    squeeze = jnp.where(a // rank == b // fields, wide, 0.0).astype(BF16)

    def reduce_chunk(c):
        loads[c].wait()
        for g in range(blocks):
            src = (c * blocks + g) * group * fields
            dst = (c * blocks + g) * group * rank
            own[dst : dst + group * rank, :] = dot(
                squeeze, emb[src : src + group * fields, :]
            ).astype(BF16)

    sends = []

    def send_chunk(c):
        rng = pl.ds(c * part * rank, part * rank)
        for side, target in ((0, after), (1, before)):
            copy = pltpu.make_async_remote_copy(
                src_ref=own.at[rng],
                dst_ref=near.at[side, rng],
                send_sem=near_send.at[side, c],
                recv_sem=near_recv.at[side, c],
                device_id=(seg, target, row),
                device_id_type=MESH,
            )
            copy.start()
            sends.append(copy)

    reduce_chunk(0)
    pl.semaphore_wait(barrier, len(peers) + 2)
    send_chunk(0)
    for c in range(1, chunks):
        reduce_chunk(c)
        send_chunk(c)

    weight = [flags_ref[0, o].astype(F32) for o in range(3)]
    a, b = grid_of((group * fields, group * rank))
    same_row = a // fields == b // rank
    a, b = grid_of((group * rank, span))
    repeat = (a % rank == b % rank).astype(BF16)
    a, b = grid_of((group * fields, span))
    same_field = a % fields == b // rank
    a, b = grid_of((group, group * fields))
    fold = (b // fields == a).astype(BF16)
    scale = 1.0 / math.sqrt(width)

    gats = []

    def interact(c):
        for side in range(2):
            sends[2 * c + side].wait_recv()
        for g in range(blocks):
            src = (c * blocks + g) * group * fields
            dst = (c * blocks + g) * group * rank
            rng = slice(dst, dst + group * rank)
            partner = (
                weight[0] * near[0, rng, :].astype(F32)
                + weight[1] * own[rng, :].astype(F32)
                + weight[2] * near[1, rng, :].astype(F32)
            ).astype(BF16)
            prod = dot(emb[src : src + group * fields, :], partner, ((1,), (1,)))
            prod = jnp.where(same_row, prod * scale, 0.0).astype(BF16)
            prod = jnp.where(same_field, dot(prod, repeat), 0.0).astype(BF16)
            inter[c, g * group : (g + 1) * group, :] = dot(fold, prod).astype(BF16)
        place = gathered.at[
            c,
            pl.ds(pl.multiple_of(row * part, part), part),
            pl.ds(pl.multiple_of(fld * span, span), span),
        ]
        for i, peer in enumerate(peers):
            copy = pltpu.make_async_remote_copy(
                src_ref=inter.at[c],
                dst_ref=place,
                send_sem=gat_send.at[c, i],
                recv_sem=gat_recv.at[c],
                device_id=peer,
                device_id_type=MESH,
            )
            copy.start()
            gats.append(copy)
        pltpu.make_async_copy(inter.at[c], place, gat_recv.at[c]).start()

    backs = {}

    def project(c):
        pltpu.make_async_copy(gathered.at[c], gathered.at[c], gat_recv.at[c]).wait()
        if c == 0:
            mix_load.wait()
        cols = each * width
        step = min(cols, 512)
        for n in range(0, cols, step):
            mixed[c, :, n : n + step] = dot(
                gathered[c], mix[:, n : n + step]
            ).astype(BF16)
        for j in range(1, groups):
            to = lax.rem(row + j, groups)
            copy = pltpu.make_async_remote_copy(
                src_ref=mixed.at[c, pl.ds(pl.multiple_of(to * part, part), part)],
                dst_ref=back.at[c, j - 1],
                send_sem=back_send.at[c, j - 1],
                recv_sem=back_recv.at[c, j - 1],
                device_id=(seg, fld, to),
                device_id_type=MESH,
            )
            copy.start()
            backs[c, j] = copy

    outs = []

    def finish(c):
        for j in range(groups):
            source = lax.rem(row + groups - j, groups)
            if j:
                backs[c, j].wait_recv()
            for f in range(each):
                lanes = slice(f * width, (f + 1) * width)
                if j:
                    piece = back[c, j - 1, :, lanes]
                else:
                    mine = pl.ds(pl.multiple_of(row * part, part), part)
                    piece = mixed[c, mine, lanes]
                piece = piece.astype(F32)
                for l in range(width // 128):
                    spread[l, pl.ds(source * each + f, part, stride=fields), :] = piece[
                        :, l * 128 : (l + 1) * 128
                    ]
        gain = gain_ref[...][None]
        size = 8 * fields
        for i in range(part // 8):
            at = c * part * fields + i * size
            here = slice(i * size, (i + 1) * size)
            summed = emb[at : at + size, :].astype(F32) + jnp.concatenate(
                [spread[l, here, :] for l in range(width // 128)], axis=1
            )
            mean = jnp.sum(summed * summed, axis=-1, keepdims=True) * (1.0 / width)
            normed = summed * lax.rsqrt(mean + 1e-06)
            normed = normed.reshape(8, fields, width) * gain
            done[at : at + size, :] = normed.reshape(size, width).astype(BF16)
        rng = pl.ds(c * part * fields, part * fields)
        copy = pltpu.make_async_remote_copy(
            src_ref=done.at[rng],
            dst_ref=out_ref.at[rng],
            send_sem=out_send.at[c],
            recv_sem=out_recv.at[c],
            device_id=ahead,
            device_id_type=MESH,
        )
        copy.start()
        outs.append(copy)

    for c in range(chunks + 2):
        if c < chunks:
            interact(c)
        if 0 <= c - 2:
            finish(c - 2)
        if 0 <= c - 1 < chunks:
            project(c - 1)

    for copy in sends:
        copy.wait_send()
    for copy in gats:
        copy.wait_send()
    for copy in backs.values():
        copy.wait_send()
    for copy in outs:
        copy.wait()


def shards(embeddings, compress, mixing, gain, flags):
    _, rows, fields, width = embeddings.shape
    segments, owners, groups = (lax.axis_size(n) for n in ("segment", "field", "row"))
    rank = compress.shape[2]
    chunks, group = 4, 16
    part = rows // chunks
    depth, cols = mixing.shape[1:]
    sizes = (segments, owners, groups, rows, fields, width, rank, chunks, group)
    vmem = pl.BlockSpec(memory_space=pltpu.VMEM)
    hbm = pl.BlockSpec(memory_space=pl.ANY)
    dma = pltpu.SemaphoreType.DMA
    others = max(groups - 1, 1)
    out = pl.pallas_call(
        functools.partial(kernel, sizes),
        out_shape=jax.ShapeDtypeStruct((rows * fields, width), BF16),
        in_specs=[hbm, vmem, hbm, vmem, pl.BlockSpec(memory_space=pltpu.SMEM)],
        out_specs=hbm,
        scratch_shapes=[
            pltpu.VMEM((rows * fields, width), BF16),
            pltpu.VMEM((depth, cols), BF16),
            pltpu.VMEM((rows * rank, width), BF16),
            pltpu.VMEM((2, rows * rank, width), BF16),
            pltpu.VMEM((chunks, part, fields * rank), BF16),
            pltpu.VMEM((chunks, groups * part, depth), BF16),
            pltpu.VMEM((chunks, groups * part, cols), BF16),
            pltpu.VMEM((chunks, others, part, cols), BF16),
            pltpu.VMEM((width // 128, part * fields, 128), F32),
            pltpu.VMEM((rows * fields, width), BF16),
            dma((chunks,)),
            dma,
            dma((2, chunks)),
            dma((2, chunks)),
            dma((chunks, owners * groups - 1)),
            dma((chunks,)),
            dma((chunks, others)),
            dma((chunks, others)),
            dma((chunks,)),
            dma((chunks,)),
        ],
        compiler_params=pltpu.CompilerParams(
            collective_id=0, has_side_effects=True, vmem_limit_bytes=48 * 2**20
        ),
    )(
        embeddings.reshape(rows * fields, width),
        compress[0],
        mixing[0],
        gain[0],
        flags,
    )
    return out.reshape(1, rows, fields, width)


def solution(mesh):
    placed = (
        P("segment", "row", "field", None),
        P("segment", None, None),
        P("segment", None, ("field", "row")),
        P("segment", "field", None),
        P("field", None),
    )
    return jax.shard_map(
        shards,
        mesh=mesh,
        in_specs=placed,
        out_specs=P("segment", "row", "field", None),
        check_vma=False,
    )
```

```python
import functools
import math

import jax
import jax.numpy as jnp
from jax import lax
from jax.experimental import pallas as pl
from jax.experimental.pallas import tpu as pltpu
from jax.sharding import PartitionSpec as P

AHEAD = 1
MESH = pl.DeviceIdType.MESH
BF16, F32 = jnp.bfloat16, jnp.float32


def dot(a, b, dims=((1,), (0,))):
    return lax.dot_general(a, b, (dims, ((), ())), preferred_element_type=F32)


def grid_of(shape):
    return (
        lax.broadcasted_iota(jnp.int32, shape, 0),
        lax.broadcasted_iota(jnp.int32, shape, 1),
    )


def kernel(
    sizes,
    emb_hbm, compress_hbm, mix_hbm, gain_hbm, flags_hbm,
    out_ref,
    emb, compress_ref, mix, gain_ref, flags_ref, own, near, inter, gathered, mixed, back, spread, done,
    emb_sem, mix_sem, small_sem,
    near_send, near_recv,
    gat_send, gat_recv,
    back_send, back_recv,
    out_send, out_recv,
):
    segments, owners, groups, rows, fields, width, rank, chunks, group = sizes
    seg = lax.axis_index("segment")
    fld = lax.axis_index("field")
    row = lax.axis_index("row")
    part = rows // chunks
    span = fields * rank
    each = fields // groups
    blocks = part // group
    before, after = lax.rem(fld + owners - 1, owners), lax.rem(fld + 1, owners)

    smalls = [
        pltpu.make_async_copy(src, dst, small_sem.at[i])
        for i, (src, dst) in enumerate(
            (
                (compress_hbm, compress_ref),
                (gain_hbm, gain_ref),
                (flags_hbm, flags_ref),
            )
        )
    ]
    for load in smalls:
        load.start()
    loads = []
    for c in range(chunks):
        rng = pl.ds(c * part * fields, part * fields)
        load = pltpu.make_async_copy(emb_hbm.at[rng], emb.at[rng], emb_sem.at[c])
        load.start()
        loads.append(load)
    mix_load = pltpu.make_async_copy(mix_hbm, mix, mix_sem)
    mix_load.start()

    barrier = pltpu.get_barrier_semaphore()
    peers = []
    for i in range(owners):
        for j in range(groups):
            if i or j:
                peers.append((seg, lax.rem(fld + i, owners), lax.rem(row + j, groups)))
    for peer in peers:
        pl.semaphore_signal(barrier, inc=1, device_id=peer, device_id_type=MESH)
    ahead = (lax.rem(seg + 1, segments), fld, row)
    behind = (lax.rem(seg + segments - 1, segments), fld, row)
    for peer in (ahead, behind):
        pl.semaphore_signal(barrier, inc=1, device_id=peer, device_id_type=MESH)

    a, b = grid_of((compress_ref.shape[1], group * fields))
    pick = (a == fld * fields + b % fields).astype(BF16)
    a, b = grid_of((group * rank, rank))
    repeat = (a % rank == b).astype(BF16)
    smalls[0].wait()
    wide = dot(repeat, dot(compress_ref[...], pick).astype(BF16))
    a, b = grid_of((group * rank, group * fields))
    squeeze = jnp.where(a // rank == b // fields, wide, 0.0).astype(BF16)

    def reduce_chunk(c):
        loads[c].wait()
        for g in range(blocks):
            src = (c * blocks + g) * group * fields
            dst = (c * blocks + g) * group * rank
            own[dst : dst + group * rank, :] = dot(
                squeeze, emb[src : src + group * fields, :]
            ).astype(BF16)

    sends = []

    def send_chunk(c):
        rng = pl.ds(c * part * rank, part * rank)
        for side, target in ((0, after), (1, before)):
            copy = pltpu.make_async_remote_copy(
                src_ref=own.at[rng],
                dst_ref=near.at[side, rng],
                send_sem=near_send.at[side, c],
                recv_sem=near_recv.at[side, c],
                device_id=(seg, target, row),
                device_id_type=MESH,
            )
            copy.start()
            sends.append(copy)

    reduce_chunk(0)
    pl.semaphore_wait(barrier, len(peers) + 2)
    send_chunk(0)
    for c in range(1, chunks):
        reduce_chunk(c)
        if c < AHEAD:
            send_chunk(c)

    smalls[2].wait()
    weight = [flags_ref[0, o].astype(F32) for o in range(3)]
    a, b = grid_of((group * fields, group * rank))
    same_row = a // fields == b // rank
    a, b = grid_of((group * rank, span))
    repeat = (a % rank == b % rank).astype(BF16)
    a, b = grid_of((group * fields, span))
    same_field = a % fields == b // rank
    a, b = grid_of((group, group * fields))
    fold = (b // fields == a).astype(BF16)
    scale = 1.0 / math.sqrt(width)

    gats = []

    def interact(c):
        for side in range(2):
            sends[2 * c + side].wait_recv()
        if c + AHEAD < chunks:
            for side in range(2):
                sends[2 * c + side].wait_send()
            send_chunk(c + AHEAD)
        for g in range(blocks):
            src = (c * blocks + g) * group * fields
            dst = (c * blocks + g) * group * rank
            rng = slice(dst, dst + group * rank)
            partner = (
                weight[0] * near[0, rng, :].astype(F32)
                + weight[1] * own[rng, :].astype(F32)
                + weight[2] * near[1, rng, :].astype(F32)
            ).astype(BF16)
            prod = dot(emb[src : src + group * fields, :], partner, ((1,), (1,)))
            prod = jnp.where(same_row, prod * scale, 0.0).astype(BF16)
            prod = jnp.where(same_field, dot(prod, repeat), 0.0).astype(BF16)
            inter[c, g * group : (g + 1) * group, :] = dot(fold, prod).astype(BF16)
        place = gathered.at[
            c,
            pl.ds(pl.multiple_of(row * part, part), part),
            pl.ds(pl.multiple_of(fld * span, span), span),
        ]
        for i, peer in enumerate(peers):
            copy = pltpu.make_async_remote_copy(
                src_ref=inter.at[c],
                dst_ref=place,
                send_sem=gat_send.at[c, i],
                recv_sem=gat_recv.at[c],
                device_id=peer,
                device_id_type=MESH,
            )
            copy.start()
            gats.append(copy)
        pltpu.make_async_copy(inter.at[c], place, gat_recv.at[c]).start()

    backs = {}

    def project(c):
        pltpu.make_async_copy(gathered.at[c], gathered.at[c], gat_recv.at[c]).wait()
        if c == 0:
            mix_load.wait()
            smalls[1].wait()
        cols = each * width
        step = min(cols, 512)
        for n in range(0, cols, step):
            mixed[c, :, n : n + step] = dot(
                gathered[c], mix[:, n : n + step]
            ).astype(BF16)
        for j in range(1, groups):
            to = lax.rem(row + j, groups)
            copy = pltpu.make_async_remote_copy(
                src_ref=mixed.at[c, pl.ds(pl.multiple_of(to * part, part), part)],
                dst_ref=back.at[c, j - 1],
                send_sem=back_send.at[c, j - 1],
                recv_sem=back_recv.at[c, j - 1],
                device_id=(seg, fld, to),
                device_id_type=MESH,
            )
            copy.start()
            backs[c, j] = copy

    outs = []

    def finish(c):
        for j in range(groups):
            source = lax.rem(row + groups - j, groups)
            if j:
                backs[c, j].wait_recv()
            for f in range(each):
                lanes = slice(f * width, (f + 1) * width)
                if j:
                    piece = back[c, j - 1, :, lanes]
                else:
                    mine = pl.ds(pl.multiple_of(row * part, part), part)
                    piece = mixed[c, mine, lanes]
                piece = piece.astype(F32)
                for l in range(width // 128):
                    spread[l, pl.ds(source * each + f, part, stride=fields), :] = piece[
                        :, l * 128 : (l + 1) * 128
                    ]
        gain = gain_ref[...][None]
        size = 8 * fields
        for i in range(part // 8):
            at = c * part * fields + i * size
            here = slice(i * size, (i + 1) * size)
            summed = emb[at : at + size, :].astype(F32) + jnp.concatenate(
                [spread[l, here, :] for l in range(width // 128)], axis=1
            )
            mean = jnp.sum(summed * summed, axis=-1, keepdims=True) * (1.0 / width)
            normed = summed * lax.rsqrt(mean + 1e-06)
            normed = normed.reshape(8, fields, width) * gain
            done[at : at + size, :] = normed.reshape(size, width).astype(BF16)
        rng = pl.ds(c * part * fields, part * fields)
        copy = pltpu.make_async_remote_copy(
            src_ref=done.at[rng],
            dst_ref=out_ref.at[rng],
            send_sem=out_send.at[c],
            recv_sem=out_recv.at[c],
            device_id=ahead,
            device_id_type=MESH,
        )
        copy.start()
        outs.append(copy)

    for c in range(chunks + 2):
        if c < chunks:
            interact(c)
        if 0 <= c - 2:
            finish(c - 2)
        if 0 <= c - 1 < chunks:
            project(c - 1)

    for copy in sends[-2 * AHEAD :]:
        copy.wait_send()
    for copy in gats:
        copy.wait_send()
    for copy in backs.values():
        copy.wait_send()
    for copy in outs:
        copy.wait()


def shards(embeddings, compress, mixing, gain, flags):
    _, rows, fields, width = embeddings.shape
    segments, owners, groups = (lax.axis_size(n) for n in ("segment", "field", "row"))
    rank = compress.shape[2]
    chunks, group = 4, 16
    part = rows // chunks
    depth, cols = mixing.shape[1:]
    sizes = (segments, owners, groups, rows, fields, width, rank, chunks, group)
    hbm = pl.BlockSpec(memory_space=pl.ANY)
    dma = pltpu.SemaphoreType.DMA
    others = max(groups - 1, 1)
    out = pl.pallas_call(
        functools.partial(kernel, sizes),
        out_shape=jax.ShapeDtypeStruct((rows * fields, width), BF16),
        in_specs=[hbm] * 5,
        out_specs=hbm,
        scratch_shapes=[
            pltpu.VMEM((rows * fields, width), BF16),
            pltpu.VMEM((rank, compress.shape[1]), BF16),
            pltpu.VMEM((depth, cols), BF16),
            pltpu.VMEM((fields, width), F32),
            pltpu.SMEM(flags.shape, jnp.int32),
            pltpu.VMEM((rows * rank, width), BF16),
            pltpu.VMEM((2, rows * rank, width), BF16),
            pltpu.VMEM((chunks, part, fields * rank), BF16),
            pltpu.VMEM((chunks, groups * part, depth), BF16),
            pltpu.VMEM((chunks, groups * part, cols), BF16),
            pltpu.VMEM((chunks, others, part, cols), BF16),
            pltpu.VMEM((width // 128, part * fields, 128), F32),
            pltpu.VMEM((rows * fields, width), BF16),
            dma((chunks,)),
            dma,
            dma((3,)),
            dma((2, chunks)),
            dma((2, chunks)),
            dma((chunks, owners * groups - 1)),
            dma((chunks,)),
            dma((chunks, others)),
            dma((chunks, others)),
            dma((chunks,)),
            dma((chunks,)),
        ],
        compiler_params=pltpu.CompilerParams(
            collective_id=0, has_side_effects=True, vmem_limit_bytes=60 * 2**20
        ),
    )(
        embeddings.reshape(rows * fields, width),
        compress[0].T,
        mixing[0],
        gain[0],
        flags,
    )
    return out.reshape(1, rows, fields, width)


def solution(mesh):
    placed = (
        P("segment", "row", "field", None),
        P("segment", None, None),
        P("segment", None, ("field", "row")),
        P("segment", "field", None),
        P("field", None),
    )
    return jax.shard_map(
        shards,
        mesh=mesh,
        in_specs=placed,
        out_specs=P("segment", "row", "field", None),
        check_vma=False,
    )
```

```python
import functools
import math

import jax
import jax.numpy as jnp
from jax import lax
from jax.experimental import pallas as pl
from jax.experimental.pallas import tpu as pltpu
from jax.sharding import PartitionSpec as P

AHEAD = 2
CHUNK = 32
MESH = pl.DeviceIdType.MESH
BF16, F32 = jnp.bfloat16, jnp.float32


def dot(a, b, dims=((1,), (0,))):
    return lax.dot_general(a, b, (dims, ((), ())), preferred_element_type=F32)


def grid_of(shape):
    return (
        lax.broadcasted_iota(jnp.int32, shape, 0),
        lax.broadcasted_iota(jnp.int32, shape, 1),
    )


def kernel(
    sizes, parts,
    emb_hbm, compress_hbm, mix_hbm, gain_hbm, flags_hbm,
    out_ref,
    emb, compress_ref, mix, gain_ref, flags_ref,
    own, near, inter, gathered, mixed, back, spread, done,
    emb_sem, mix_sem, small_sem,
    near_send, near_recv,
    gat_send, gat_recv,
    back_send, back_recv,
    out_send, out_recv,
):
    segments, owners, groups, rows, fields, width, rank, group = sizes
    seg = lax.axis_index("segment")
    fld = lax.axis_index("field")
    row = lax.axis_index("row")
    span = fields * rank
    each = fields // groups
    tall_in, tall_out = group * fields, group * rank
    pieces = rows // group
    before, after = lax.rem(fld + owners - 1, owners), lax.rem(fld + 1, owners)

    smalls = [
        pltpu.make_async_copy(src, dst, small_sem.at[i])
        for i, (src, dst) in enumerate(
            (
                (compress_hbm, compress_ref),
                (gain_hbm, gain_ref),
                (flags_hbm, flags_ref),
            )
        )
    ]
    for load in smalls:
        load.start()
    loads = []
    for p in range(pieces):
        rng = pl.ds(p * tall_in, tall_in)
        load = pltpu.make_async_copy(emb_hbm.at[rng], emb.at[rng], emb_sem.at[p])
        load.start()
        loads.append(load)
    mix_load = pltpu.make_async_copy(mix_hbm, mix, mix_sem)
    mix_load.start()

    barrier = pltpu.get_barrier_semaphore()
    ahead = (lax.rem(seg + 1, segments), fld, row)
    behind = (lax.rem(seg + segments - 1, segments), fld, row)
    peers = [
        (seg, lax.rem(fld + i, owners), lax.rem(row + j, groups))
        for i in range(owners)
        for j in range(groups)
        if i or j
    ]
    greeted = peers + [ahead, behind]
    for peer in greeted:
        pl.semaphore_signal(barrier, inc=1, device_id=peer, device_id_type=MESH)

    a, b = grid_of((compress_ref.shape[1], tall_in))
    pick = (a == fld * fields + b % fields).astype(BF16)
    a, b = grid_of((tall_out, rank))
    repeat = (a % rank == b).astype(BF16)
    smalls[0].wait()
    wide = dot(repeat, dot(compress_ref[...], pick).astype(BF16))
    a, b = grid_of((tall_out, tall_in))
    squeeze = jnp.where(a // rank == b // fields, wide, 0.0).astype(BF16)

    def reduce_piece(p):
        loads[p].wait()
        own[p * tall_out : (p + 1) * tall_out, :] = dot(
            squeeze, emb[p * tall_in : (p + 1) * tall_in, :]
        ).astype(BF16)

    sends = []

    def send_piece(p):
        rng = pl.ds(p * tall_out, tall_out)
        for side, target in ((0, after), (1, before)):
            copy = pltpu.make_async_remote_copy(
                src_ref=own.at[rng],
                dst_ref=near.at[side, rng],
                send_sem=near_send.at[side, p],
                recv_sem=near_recv.at[side, p],
                device_id=(seg, target, row),
                device_id_type=MESH,
            )
            copy.start()
            sends.append(copy)

    reduce_piece(0)
    pl.semaphore_wait(barrier, len(greeted))
    send_piece(0)
    for p in range(1, pieces):
        reduce_piece(p)
        if p < AHEAD:
            send_piece(p)

    smalls[2].wait()
    weight = [flags_ref[0, o].astype(F32) for o in range(3)]
    a, b = grid_of((tall_in, tall_out))
    same_row = a // fields == b // rank
    a, b = grid_of((tall_out, span))
    repeat = (a % rank == b % rank).astype(BF16)
    a, b = grid_of((tall_in, span))
    same_field = a % fields == b // rank
    a, b = grid_of((group, tall_in))
    fold = (b // fields == a).astype(BF16)
    scale = 1.0 / math.sqrt(width)

    def place_of(c, source):
        first, part = parts[c]
        at = groups * first + source * part
        return pl.ds(pl.multiple_of(at, group), part)

    columns = pl.ds(pl.multiple_of(fld * span, span), span)

    def interact(c, p):
        for side in range(2):
            sends[2 * p + side].wait_recv()
        if p + AHEAD < pieces:
            for side in range(2):
                sends[2 * p + side].wait_send()
            send_piece(p + AHEAD)
        rng = slice(p * tall_out, (p + 1) * tall_out)
        partner = (
            weight[0] * near[0, rng, :].astype(F32)
            + weight[1] * own[rng, :].astype(F32)
            + weight[2] * near[1, rng, :].astype(F32)
        ).astype(BF16)
        prod = dot(emb[p * tall_in : (p + 1) * tall_in, :], partner, ((1,), (1,)))
        prod = jnp.where(same_row, prod * scale, 0.0).astype(BF16)
        prod = jnp.where(same_field, dot(prod, repeat), 0.0).astype(BF16)
        inter[p * group : (p + 1) * group, :] = dot(fold, prod).astype(BF16)

    gats = []

    def gather(c):
        piece = inter.at[pl.ds(*parts[c])]
        slot = gathered.at[place_of(c, row), columns]
        pltpu.make_async_copy(piece, slot, gat_recv.at[c]).start()
        for i, peer in enumerate(peers):
            copy = pltpu.make_async_remote_copy(
                src_ref=piece,
                dst_ref=slot,
                send_sem=gat_send.at[c, i],
                recv_sem=gat_recv.at[c],
                device_id=peer,
                device_id_type=MESH,
            )
            copy.start()
            gats.append(copy)

    backs = {}

    def project(c):
        if c == 0:
            mix_load.wait()
            smalls[1].wait()
        first, part = parts[c]
        cols = each * width
        step = min(cols, 512)
        here = slice(groups * first, groups * (first + part))
        whole = gathered.at[pl.ds(groups * first, groups * part)]
        pltpu.make_async_copy(whole, whole, gat_recv.at[c]).wait()
        for n in range(0, cols, step):
            mixed[here, n : n + step] = dot(
                gathered[here, :], mix[:, n : n + step]
            ).astype(BF16)
        for j in range(1, groups):
            to = lax.rem(row + j, groups)
            copy = pltpu.make_async_remote_copy(
                src_ref=mixed.at[place_of(c, to)],
                dst_ref=back.at[j - 1, pl.ds(first, part)],
                send_sem=back_send.at[c, j - 1],
                recv_sem=back_recv.at[c, j - 1],
                device_id=(seg, fld, to),
                device_id_type=MESH,
            )
            copy.start()
            backs[c, j] = copy

    outs = []

    def finish(c):
        first, part = parts[c]
        for j in range(groups):
            source = lax.rem(row + groups - j, groups)
            if j:
                backs[c, j].wait_recv()
            for f in range(each):
                lanes = slice(f * width, (f + 1) * width)
                if j:
                    piece = back[j - 1, first : first + part, lanes]
                else:
                    piece = mixed[place_of(c, row), lanes]
                piece = piece.astype(F32)
                for l in range(width // 128):
                    spread[l, pl.ds(source * each + f, part, stride=fields), :] = piece[
                        :, l * 128 : (l + 1) * 128
                    ]
        gain = gain_ref[...][None]
        size = 8 * fields
        for i in range(part // 8):
            at = first * fields + i * size
            here = slice(i * size, (i + 1) * size)
            summed = emb[at : at + size, :].astype(F32) + jnp.concatenate(
                [spread[l, here, :] for l in range(width // 128)], axis=1
            )
            mean = jnp.sum(summed * summed, axis=-1, keepdims=True) * (1.0 / width)
            normed = summed * lax.rsqrt(mean + 1e-06)
            normed = normed.reshape(8, fields, width) * gain
            done[at : at + size, :] = normed.reshape(size, width).astype(BF16)
        rng = pl.ds(first * fields, part * fields)
        copy = pltpu.make_async_remote_copy(
            src_ref=done.at[rng],
            dst_ref=out_ref.at[rng],
            send_sem=out_send.at[c],
            recv_sem=out_recv.at[c],
            device_id=ahead,
            device_id_type=MESH,
        )
        copy.start()
        outs.append(copy)

    last = len(parts) - 1
    for c, (first, part) in enumerate(parts):
        early = part > group
        for p in range(first // group, (first + part) // group):
            interact(c, p)
        gather(c)
        if c >= 2:
            finish(c - 2)
        if c:
            project(c - 1)
    if last:
        finish(last - 1)
    project(last)
    finish(last)

    for copy in sends[-2 * AHEAD :] + gats:
        copy.wait_send()
    for copy in backs.values():
        copy.wait_send()
    for copy in outs:
        copy.wait()


def shards(embeddings, compress, mixing, gain, flags):
    _, rows, fields, width = embeddings.shape
    segments, owners, groups = (lax.axis_size(n) for n in ("segment", "field", "row"))
    rank = compress.shape[2]
    group = 16
    depth, cols = mixing.shape[1:]
    parts, first = [], 0
    while first < rows:
        part = min(CHUNK, rows - first)
        parts.append((first, part))
        first += part
    chunks, pieces = len(parts), rows // group
    sizes = (segments, owners, groups, rows, fields, width, rank, group)
    hbm = pl.BlockSpec(memory_space=pl.ANY)
    dma = pltpu.SemaphoreType.DMA
    others = max(groups - 1, 1)
    out = pl.pallas_call(
        functools.partial(kernel, sizes, parts),
        out_shape=jax.ShapeDtypeStruct((rows * fields, width), BF16),
        in_specs=[hbm] * 5,
        out_specs=pl.BlockSpec(memory_space=pl.ANY),
        scratch_shapes=[
            pltpu.VMEM((rows * fields, width), BF16),
            pltpu.VMEM((rank, compress.shape[1]), BF16),
            pltpu.VMEM((depth, cols), BF16),
            pltpu.VMEM((fields, width), F32),
            pltpu.SMEM(flags.shape, jnp.int32),
            pltpu.VMEM((rows * rank, width), BF16),
            pltpu.VMEM((2, rows * rank, width), BF16),
            pltpu.VMEM((rows, fields * rank), BF16),
            pltpu.VMEM((groups * rows, depth), BF16),
            pltpu.VMEM((groups * rows, cols), BF16),
            pltpu.VMEM((others, rows, cols), BF16),
            pltpu.VMEM((width // 128, CHUNK * fields, 128), F32),
            pltpu.VMEM((rows * fields, width), BF16),
            dma((pieces,)),
            dma,
            dma((3,)),
            dma((2, pieces)),
            dma((2, pieces)),
            dma((chunks, owners * groups - 1)),
            dma((chunks,)),
            dma((chunks, others)),
            dma((chunks, others)),
            dma((chunks,)),
            dma((chunks,)),
        ],
        compiler_params=pltpu.CompilerParams(
            collective_id=0, has_side_effects=True, vmem_limit_bytes=60 * 2**20
        ),
    )(
        embeddings.reshape(rows * fields, width),
        compress[0].T,
        mixing[0],
        gain[0],
        flags,
    )
    return out.reshape(1, rows, fields, width)


def solution(mesh):
    placed = (
        P("segment", "row", "field", None),
        P("segment", None, None),
        P("segment", None, ("field", "row")),
        P("segment", "field", None),
        P("field", None),
    )
    return jax.shard_map(
        shards,
        mesh=mesh,
        in_specs=placed,
        out_specs=P("segment", "row", "field", None),
        check_vma=False,
    )
```
